32 devices in a mesh: groups: 2 (over y), pipe: 16 (over z, x, core).
Axes of the slice: x: 2, y: 2, z: 4, core: 2. Of those that a mesh axis runs over, the one named last changes fastest.
Arguments:
- hidden: bfloat16 [256, 18432], P(('groups', 'pipe')), parts along dimension 0, may hold values from -128 to 128
- head_rows: bfloat16 [4096, 18432], P(('groups', 'pipe')), parts along dimension 0, may hold values from -1 to 1
- teacher: bfloat16 [256, 2048], P('groups', 'pipe'), parts along dimension 0, may hold values from -240 to 240
- targets: int32 [256], P('groups'), parts along dimension 0, may hold values from 0 to 2047
- token_weight: float32 [256], P('groups'), parts along dimension 0, may hold values from 0.5 to 2
Outputs:
- loss: float32 [256], P(('groups', 'pipe')), parts along dimension 0
- grad_hidden: bfloat16 [256, 18432], P(('groups', 'pipe')), parts along dimension 0
- grad_head: bfloat16 [4096, 18432], P(('groups', 'pipe')), parts along dimension 0
The draws below stay inside these ranges and needn't reach their ends.
There are 2 independent parts, one for each index of `groups`. The reference program is written for one: setup_inputs(seed, part) draws one part's arguments, and reference() takes and returns one part's arrays. A program takes and returns all parts, laid end to end along the dimension named above; each array names one. Nothing has to cross between parts.
All inputs are finite; a program needn't handle non-finite values.
Results may differ from the reference program's by a relative error of at most 0.0051.
Values may be sent and summed in bfloat16 or wider, within the bound.
No kernel may reach another device: no remote copies, remote signals or barrier semaphores. Data moves between devices by JAX's collectives and lax.ppermute only.
A program may use at most 128 MiB of HBM per device.

```python
import math
import jax
import jax.numpy as jnp

D = 18432
TOKENS = 128
NEGATIVES = 2048


def head_table(key):
    values = jax.random.normal(key, (NEGATIVES, D), jnp.float32)
    return jnp.clip(values, -6.0, 6.0) * D ** (-0.5)


def draw_head_rows(key, part):
    table = head_table(key)
    return table.astype(jnp.bfloat16)


def draw_hidden(key, part):
    key = jax.random.fold_in(key, 2)
    base_key = jax.random.fold_in(key, 0)
    base = jnp.clip(jax.random.normal(base_key, (TOKENS, D), jnp.float32), -6.0, 6.0)
    return base.astype(jnp.bfloat16)


def draw_teacher(key, part):
    key = jax.random.fold_in(key, 3)
    base_key = jax.random.fold_in(key, 0)
    base = jnp.clip(3.0 * jax.random.normal(base_key, (TOKENS, NEGATIVES), jnp.float32), -15.0, 15.0)
    return base.astype(jnp.bfloat16)


def plant(values, stream_key, smallest, top_value):
    spot = [jax.random.randint(jax.random.fold_in(stream_key, axis), (), 0, length) for axis, length in enumerate(values.shape)]
    main_axis = values.shape.index(max(values.shape))
    beside = spot[:main_axis] + [(spot[main_axis] + 1) % values.shape[main_axis]] + spot[main_axis + 1:]
    return values.at[tuple(spot)].set(smallest).at[tuple(beside)].set(top_value)


def setup_inputs(seed: int = 0, part: int = 0) -> dict:
    splits = jax.random.split(jax.random.key(seed), 6)
    own_keys = jax.random.split(jax.random.fold_in(splits[5], part), 6)
    hidden = draw_hidden(jax.random.fold_in(jax.random.fold_in(splits[5], part), 71), part)
    head_rows = draw_head_rows(jax.random.fold_in(jax.random.fold_in(splits[5], part), 71), part)
    teacher = draw_teacher(jax.random.fold_in(jax.random.fold_in(splits[5], part), 71), part)
    targets = plant(jax.random.randint(own_keys[3], (TOKENS,), 0, NEGATIVES), jax.random.fold_in(own_keys[3], 1), 0, NEGATIVES - 1).astype(jnp.int32)
    token_weight = jnp.clip(jnp.exp(jax.random.uniform(own_keys[4], (TOKENS,), jnp.float32, math.log(0.5), math.log(2.0))), 0.5, 2.0)
    return dict(hidden=hidden, head_rows=head_rows, teacher=teacher, targets=targets, token_weight=token_weight)


def reference(hidden, head_rows, teacher, targets, token_weight):
    student = 3.0 * jnp.dot(hidden, head_rows.T, preferred_element_type=jnp.float32)
    teach = teacher.astype(jnp.float32)
    smax = jnp.max(student, axis=1)
    tmax = jnp.max(teach, axis=1)
    sexp = jnp.exp(student - smax[:, None])
    texp = jnp.exp(teach - tmax[:, None])
    szero = jnp.sum(sexp, axis=1)
    tzero = jnp.sum(texp, axis=1)
    cross = jnp.sum(texp * (teach - student), axis=1)
    onehot = (targets[:, None] == jnp.arange(NEGATIVES, dtype=jnp.int32)[None, :]).astype(student.dtype)
    picked = jnp.sum(onehot * student, axis=1)
    slog = smax + jnp.log(szero)
    tlog = tmax + jnp.log(tzero)
    loss = cross / tzero - tlog + 2.0 * slog - picked
    dlogit = (3.0 * token_weight[:, None] * (2.0 * sexp / szero[:, None] - texp / tzero[:, None] - onehot)).astype(jnp.bfloat16)
    grad_hidden = jnp.dot(dlogit, head_rows, preferred_element_type=jnp.float32).astype(jnp.bfloat16)
    grad_head = jnp.dot(dlogit.T, hidden, preferred_element_type=jnp.float32).astype(jnp.bfloat16)
    return loss, grad_hidden, grad_head
```

```python
import jax
import jax.numpy as jnp
from jax import lax
from jax.sharding import PartitionSpec as P

F32 = jnp.float32
BF16 = jnp.bfloat16


def chip_ring(chips):
    return list(range(0, chips, 2)) + list(reversed(range(1, chips, 2)))


def ring_shift(ring, by):
    n = len(ring)
    return [(2 * ring[i] + c, 2 * ring[(i + by) % n] + c) for i in range(n) for c in (0, 1)]


def swap_pairs(devices, mask):
    return [(i, i ^ mask) for i in range(devices)]


def merge(a, b):
    sm = jnp.maximum(a[0], b[0])
    tm = jnp.maximum(a[1], b[1])
    sa, sb = jnp.exp(a[0] - sm), jnp.exp(b[0] - sm)
    ta, tb = jnp.exp(a[1] - tm), jnp.exp(b[1] - tm)
    return jnp.stack(
        [sm, tm, a[2] * sa + b[2] * sb, a[3] * ta + b[3] * tb, a[4] * ta + b[4] * tb, a[5] + b[5]]
    )


def local_stats(student, teach, onehot):
    sm = jnp.max(student, axis=1)
    tm = jnp.max(teach, axis=1)
    sexp = jnp.exp(student - sm[:, None])
    texp = jnp.exp(teach - tm[:, None])
    return jnp.stack(
        [
            sm,
            tm,
            jnp.sum(sexp, axis=1),
            jnp.sum(texp, axis=1),
            jnp.sum(texp * (teach - student), axis=1),
            jnp.sum(onehot * student, axis=1),
        ]
    )


def roll_to(x, shift, axis):
    size = x.shape[axis]
    return lax.dynamic_slice_in_dim(jnp.concatenate([x, x], axis), shift, size, axis)


def program(devices, hidden, head_rows, teacher, targets, token_weight):
    chips = devices // 2
    ring = chip_ring(chips)
    far = chips // 2
    tokens, width = hidden.shape
    ids = head_rows.shape[0]
    half = width // 2
    block = 2 * tokens
    total = chips * block

    me = lax.axis_index("pipe")
    core = me % 2
    chip = me // 2
    place = jnp.where(chip % 2 == 0, chip // 2, chips - 1 - chip // 2)
    to_core = swap_pairs(devices, 1)
    right, left = ring_shift(ring, 1), ring_shift(ring, -1)

    def send(x, perm):
        return lax.ppermute(x, "pipe", perm)

    def my_half(x):
        return lax.dynamic_slice_in_dim(x, core * half, half, 1)

    def other_half(x):
        return lax.dynamic_slice_in_dim(x, (1 - core) * half, half, 1)

    mine = my_half(hidden)
    theirs = send(other_half(hidden), to_core)
    block0 = jnp.where(
        core == 0, jnp.concatenate([mine, theirs]), jnp.concatenate([theirs, mine])
    )
    own_head = my_half(head_rows)
    sib_head = send(other_half(head_rows), to_core)

    blocks = {0: block0}
    from_left = from_right = block0
    for step in range(1, far):
        from_left = send(from_left, right)
        from_right = send(from_right, left)
        blocks[-step] = from_left
        blocks[step] = from_right
    quarter = half // 2
    blocks[far] = jnp.concatenate(
        [send(from_left[:, :quarter], right), send(from_right[:, quarter:], left)], axis=1
    )
    order = list(range(0, far + 1)) + list(range(1 - far, 0))
    whole = jnp.concatenate([blocks[k] for k in order])

    def by_distance(x):
        parts = [x[block * c : block * (c + 1)] for c in ring]
        return roll_to(jnp.concatenate(parts), place * block, 0)

    sib_teacher = send(teacher, to_core)
    teach = by_distance(jnp.concatenate([teacher, sib_teacher], axis=1)).astype(F32)
    target = by_distance(targets)
    weight = by_distance(token_weight)
    lanes = jnp.arange(ids, dtype=jnp.int32)
    columns = jnp.concatenate([me * ids + lanes, (me ^ 1) * ids + lanes])
    onehot = (target[:, None] == columns[None, :]).astype(F32)

    def logits(x, w):
        return lax.dot_general(x, w, (((1,), (1,)), ((), ())), preferred_element_type=F32)

    own_part, sib_part = logits(whole, own_head), logits(whole, sib_head)
    swapped = send(jnp.concatenate([sib_part, own_part], axis=1), to_core)
    student = 3.0 * (jnp.concatenate([own_part, sib_part], axis=1) + swapped)

    stats = local_stats(student, teach, onehot)
    stats = roll_to(stats, (chips - place) * block % total, 1)
    mask = 2
    while mask < devices:
        stats = merge(stats, send(stats, swap_pairs(devices, mask)))
        mask *= 2
    stats = roll_to(stats, place * block, 1)
    smax, tmax, szero, tzero, cross, picked = [stats[i] for i in range(6)]
    loss_rows = cross / tzero - (tmax + jnp.log(tzero)) + 2.0 * (smax + jnp.log(szero)) - picked
    loss = lax.dynamic_slice_in_dim(loss_rows[:block], core * tokens, tokens, 0)

    sexp = jnp.exp(student - smax[:, None])
    texp = jnp.exp(teach - tmax[:, None])
    dlogit = (
        3.0 * weight[:, None] * (2.0 * sexp / szero[:, None] - texp / tzero[:, None] - onehot)
    ).astype(BF16)

    both_heads = jnp.concatenate([own_head, sib_head])
    term = jnp.dot(dlogit, both_heads, preferred_element_type=F32)
    at = {k: term[block * i : block * (i + 1)] for i, k in enumerate(order)}
    at[-far] = at[far]
    to_right = send(at[far][:, :quarter].astype(BF16), right)
    to_left = send(at[far][:, quarter:].astype(BF16), left)
    for step in range(far - 1, 0, -1):
        if step == far - 1:
            went = jnp.concatenate(
                [at[step][:, :quarter] + to_right.astype(F32), at[step][:, quarter:]], axis=1
            )
            came = jnp.concatenate(
                [at[-step][:, :quarter], at[-step][:, quarter:] + to_left.astype(F32)], axis=1
            )
        else:
            went = at[step] + to_right.astype(F32)
            came = at[-step] + to_left.astype(F32)
        to_right = send(went.astype(BF16), right)
        to_left = send(came.astype(BF16), left)
    summed = (at[0] + to_right.astype(F32) + to_left.astype(F32)).astype(BF16)
    keep = lax.dynamic_slice_in_dim(summed, core * tokens, tokens, 0)
    give = lax.dynamic_slice_in_dim(summed, (1 - core) * tokens, tokens, 0)
    got = send(give, to_core)

    def both_halves(x, y):
        return jnp.where(
            core == 0, jnp.concatenate([x, y], axis=1), jnp.concatenate([y, x], axis=1)
        )

    grad_hidden = both_halves(keep, got)

    def outer(d):
        return lax.dot_general(
            d, whole, (((0,), (0,)), ((), ())), preferred_element_type=F32
        ).astype(BF16)

    grad_sib = send(outer(dlogit[:, ids:]), to_core)
    grad_head = both_halves(outer(dlogit[:, :ids]), grad_sib)
    return loss, grad_hidden, grad_head


def solution(mesh):
    devices = mesh.shape["pipe"]

    def per_device(*args):
        return program(devices, *args)

    placed = (
        P(("groups", "pipe"), None),
        P(("groups", "pipe"), None),
        P("groups", "pipe"),
        P("groups"),
        P("groups"),
    )
    return jax.shard_map(
        per_device,
        mesh=mesh,
        in_specs=placed,
        out_specs=(P(("groups", "pipe")), P(("groups", "pipe"), None), P(("groups", "pipe"), None)),
        check_vma=False,
    )
```

```python
import jax
import jax.numpy as jnp
from jax import lax
from jax.experimental import pallas as pl
from jax.experimental.pallas import tpu as pltpu
from jax.sharding import PartitionSpec as P

F32 = jnp.float32
BF16 = jnp.bfloat16


def chip_ring(chips):
    return list(range(0, chips, 2)) + list(reversed(range(1, chips, 2)))


def shift_pairs(ring, by):
    n = len(ring)
    return [(2 * ring[i] + c, 2 * ring[(i + by) % n] + c) for i in range(n) for c in (0, 1)]


def in_vmem(count):
    return [pl.BlockSpec(memory_space=pltpu.VMEM)] * count


def kernel_params():
    return pltpu.CompilerParams(vmem_limit_bytes=12 * 2**20)


def stack_heads(own, sib):
    ids, width = own.shape

    def body(own_ref, sib_ref, out_ref, sem):
        copies = [
            pltpu.make_async_copy(own_ref, out_ref.at[0:ids], sem.at[0]),
            pltpu.make_async_copy(sib_ref, out_ref.at[ids : 2 * ids], sem.at[1]),
        ]
        for c in copies:
            c.start()
        for c in copies:
            c.wait()

    return pl.pallas_call(
        body,
        out_shape=pltpu.VMEM((2 * ids, width), own.dtype),
        in_specs=[pl.BlockSpec(memory_space=pl.ANY)] * 2,
        out_specs=in_vmem(1)[0],
        scratch_shapes=[pltpu.SemaphoreType.DMA((2,))],
        compiler_params=kernel_params(),
        cost_estimate=pl.CostEstimate(
            flops=0, bytes_accessed=8 * ids * width, transcendentals=0
        ),
        name="stack_heads",
    )(own, sib)


def tile_of(width, most):
    tile = 128
    while tile * 2 <= most and width % (tile * 2) == 0:
        tile *= 2
    for factor in (3, 9):
        if tile * factor <= most and width % (tile * factor) == 0:
            return tile * factor
    return tile


def rows_of(group, start, size):
    parts = []
    for pieces in group:
        piece, at = pieces[0], start
        if start >= piece.shape[1]:
            piece, at = pieces[1], start - piece.shape[1]
        parts.append(piece[:, at : at + size])
    if len(parts) == 1:
        return parts[0]
    return jnp.concatenate([p.astype(F32) for p in parts]).astype(parts[0].dtype)


def whole_rows(group):
    return jnp.concatenate([jnp.concatenate(pieces, axis=1) for pieces in group])


def regroup(group, refs):
    refs = iter(refs)
    return [[next(refs) for _ in pieces] for pieces in group]


def logits(group, heads):
    tokens = group[0][0].shape[0]
    ids, width = heads.shape
    rows = tokens * len(group)
    if tokens % 8:
        return 3.0 * lax.dot_general(
            heads, whole_rows(group), (((1,), (1,)), ((), ())), preferred_element_type=F32
        )
    tile = tile_of(width // 2, 2304)
    flat = [x for pieces in group for x in pieces]

    def body(*refs):
        heads_ref, out_ref = refs[-2:]
        blocks = regroup(group, refs)
        acc = jnp.zeros((ids, rows), F32)
        for j in range(width // tile):
            x = rows_of(blocks, j * tile, tile)
            w = heads_ref[:, j * tile : (j + 1) * tile]
            acc += lax.dot_general(w, x, (((1,), (1,)), ((), ())), preferred_element_type=F32)
        out_ref[...] = 3.0 * acc

    return pl.pallas_call(
        body,
        out_shape=jax.ShapeDtypeStruct((ids, rows), F32),
        in_specs=in_vmem(len(flat) + 1),
        out_specs=in_vmem(1)[0],
        compiler_params=kernel_params(),
        cost_estimate=pl.CostEstimate(
            flops=2 * ids * max(rows, 256) * width,
            bytes_accessed=2 * ids * width,
            transcendentals=0,
        ),
        name="logits",
    )(*flat, heads)


def assemble(group):
    tokens, dtype = group[0][0].shape[0], group[0][0].dtype
    rows = tokens * len(group)
    width = sum(x.shape[1] for x in group[0])
    if tokens % 8:
        return whole_rows(group)
    flat = [x for pieces in group for x in pieces]

    def body(*refs):
        out_ref = refs[-1]
        blocks = regroup(group, refs)
        for start in (0, width // 2):
            for i in range(0, len(blocks), 2):
                two = blocks[i : i + 2]
                out_ref[
                    tokens * i : tokens * (i + len(two)), start : start + width // 2
                ] = rows_of(two, start, width // 2)

    return pl.pallas_call(
        body,
        out_shape=pltpu.VMEM((rows, width), dtype),
        in_specs=in_vmem(len(flat)),
        out_specs=in_vmem(1)[0],
        compiler_params=kernel_params(),
        cost_estimate=pl.CostEstimate(
            flops=0, bytes_accessed=4 * rows * width, transcendentals=0
        ),
        name="assemble",
    )(*flat)


def gradient_terms(dlogit, heads, late):
    ids, rows = dlogit.shape
    half = heads.shape[1] // 2
    early = rows - late
    if late % 8:
        term = lax.dot_general(dlogit, heads, (((0,), (0,)), ((), ())), preferred_element_type=F32)
        halves = term[:, :half], term[:, half:]
        return [h[:early] for h in halves] + [h[early:].astype(BF16) for h in halves]
    tile = tile_of(half, 1024)
    steps = half // tile

    def body(d_ref, heads_ref, *refs):
        d = d_ref[...].T
        for j in range(2 * steps):
            w = heads_ref[:, j * tile : (j + 1) * tile]
            term = jnp.dot(d, w, preferred_element_type=F32)
            cols = slice(j % steps * tile, (j % steps + 1) * tile)
            refs[j // steps][:, cols] = term[:early]
            refs[2 + j // steps][:, cols] = term[early:].astype(BF16)

    return pl.pallas_call(
        body,
        out_shape=[pltpu.VMEM((early, half), F32)] * 2 + [pltpu.VMEM((late, half), BF16)] * 2,
        in_specs=in_vmem(2),
        out_specs=in_vmem(4),
        compiler_params=kernel_params(),
        cost_estimate=pl.CostEstimate(
            flops=2 * ids * 256 * 2 * half, bytes_accessed=4 * ids * half, transcendentals=0
        ),
        name="gradient_terms",
    )(dlogit, heads)


def ring_sums(term, rows, flows):
    half = term.shape[1]
    given = [f for f in flows if f is not None]
    tokens = given[0].shape[0]

    def total(own, flow):
        return (own if flow is None else own + flow.astype(F32)).astype(BF16)

    if tokens % 8:
        return [total(term[r : r + tokens], f) for r, f in zip(rows, flows)]

    def body(term_ref, *refs):
        came = iter(refs[: len(given)])
        for i in (0, 1):
            flow = None if flows[i] is None else next(came)[...]
            refs[len(given) + i][...] = total(term_ref[rows[i] : rows[i] + tokens, :], flow)

    return pl.pallas_call(
        body,
        out_shape=[jax.ShapeDtypeStruct((tokens, half), BF16)] * 2,
        in_specs=in_vmem(1 + len(given)),
        out_specs=in_vmem(2),
        compiler_params=kernel_params(),
        cost_estimate=pl.CostEstimate(
            flops=2 * tokens * half, bytes_accessed=4 * tokens * half, transcendentals=0
        ),
        name="ring_sums",
    )(term, *given)


def local_stats(student, teach, onehot):
    sm = jnp.max(student, axis=0)
    tm = jnp.max(teach, axis=0)
    sexp = jnp.exp(student - sm)
    texp = jnp.exp(teach - tm)
    return jnp.stack(
        [
            sm,
            tm,
            jnp.sum(sexp, axis=0),
            jnp.sum(texp, axis=0),
            jnp.sum(texp * (teach - student), axis=0),
            jnp.sum(onehot * student, axis=0),
        ]
    )


def merge(every):
    sm = jnp.max(every[:, 0], axis=0)
    tm = jnp.max(every[:, 1], axis=0)
    s = jnp.exp(every[:, 0] - sm)
    t = jnp.exp(every[:, 1] - tm)
    return (
        sm,
        tm,
        jnp.sum(every[:, 2] * s, axis=0),
        jnp.sum(every[:, 3] * t, axis=0),
        jnp.sum(every[:, 4] * t, axis=0),
        jnp.sum(every[:, 5], axis=0),
    )


def from_every_chip(x, ring):
    n = len(ring)
    known = x[None]
    reach = 0
    while known.shape[0] < n:
        width = 2 * reach + 1
        missing = n - width
        right = min(width, (missing + 1) // 2)
        left = min(width, missing - right)
        ahead = lax.ppermute(known[:right], "pipe", shift_pairs(ring, -width))
        parts = [known, ahead]
        if left:
            parts.insert(0, lax.ppermute(known[width - left :], "pipe", shift_pairs(ring, width)))
        known = jnp.concatenate(parts)
        reach = 3 * reach + 1
    return known


def program(devices, hidden, head_rows, teacher, targets, token_weight):
    chips = devices // 2
    ring = chip_ring(chips)
    far = chips // 2
    tokens, width = hidden.shape
    half = width // 2
    ids = head_rows.shape[0]

    me = lax.axis_index("pipe")
    core = me % 2
    chip = me // 2
    place = jnp.where(chip % 2 == 0, chip // 2, chips - 1 - chip // 2)
    to_core = [(i, i ^ 1) for i in range(devices)]
    to_right, to_left = shift_pairs(ring, 1), shift_pairs(ring, -1)

    def send(x, perm):
        return lax.ppermute(x, "pipe", perm)

    sib_head = send(head_rows, to_core)
    heads = stack_heads(head_rows, sib_head)

    blocks = {0: hidden}
    for k in range(1, far):
        behind, ahead = blocks[1 - k], blocks[k - 1]
        if k == far - 1:
            behind, ahead, heads = lax.optimization_barrier((behind, ahead, heads))
        blocks[-k] = send(behind, to_right)
        blocks[k] = send(ahead, to_left)
    order = list(range(0, far)) + list(range(1 - far, 0)) + [far]
    order = [0] + [s * k for k in range(1, far) for s in (1, -1)] + [far]
    near = [k for k in order if abs(k) < far - 1]
    early = logits([[blocks[k]] for k in near], heads)
    rest = [k for k in order if k not in near and k != far]
    edge_left, edge_right, early = lax.optimization_barrier((blocks[1 - far], blocks[far - 1], early))
    last = (send(edge_left[:, :half], to_right), send(edge_right[:, half:], to_left))
    blocks = {k: [x] for k, x in blocks.items()}
    blocks[far] = last
    parts = [early, logits([blocks[k] for k in rest], heads), logits([blocks[far]], heads)]
    rows = len(order) * tokens

    steps = jnp.array(order, jnp.int32)
    at = (place + steps) % chips
    row_chip = jnp.where(at < chips // 2, 2 * at, 2 * (chips - 1 - at) + 1)
    inner = jnp.arange(tokens, dtype=jnp.int32)[None, :]
    row_token = (((2 * row_chip + core) * tokens)[:, None] + inner).reshape(rows)
    row_slot = ((row_chip * tokens)[:, None] + inner).reshape(rows)
    select = row_token[:, None] == jnp.arange(devices * tokens, dtype=jnp.int32)[None, :]
    slots = (row_slot[:, None] == jnp.arange(rows, dtype=jnp.int32)[None, :]).astype(F32)

    def pick(x):
        return jnp.sum(jnp.where(select, x[None, :], 0), axis=1, dtype=x.dtype)

    both_teacher = jnp.concatenate([teacher, send(teacher, to_core)], axis=1)
    teach = lax.dot_general(
        both_teacher, select.astype(BF16), (((0,), (1,)), ((), ())), preferred_element_type=F32
    )
    target = pick(targets)
    weight = pick(token_weight)
    lanes = jnp.arange(ids, dtype=jnp.int32)
    columns = jnp.concatenate([me * ids + lanes, (me ^ 1) * ids + lanes])
    onehot = (columns[:, None] == target[None, :]).astype(F32)

    student = jnp.concatenate(parts, axis=1)
    exact = lax.Precision.HIGHEST
    stats = jnp.dot(local_stats(student, teach, onehot), slots, precision=exact)
    merged = jnp.stack(merge(from_every_chip(stats, ring)))
    smax, tmax, szero, tzero, cross, picked = lax.dot_general(
        merged, slots, (((1,), (1,)), ((), ())), precision=exact
    )
    loss_rows = cross / tzero - (tmax + jnp.log(tzero)) + 2.0 * (smax + jnp.log(szero)) - picked
    loss = loss_rows[:tokens]

    sexp = jnp.exp(student - smax)
    texp = jnp.exp(teach - tmax)
    dlogit = (3.0 * weight * (2.0 * sexp / szero - texp / tzero - onehot)).astype(BF16)

    *term, first, second = gradient_terms(dlogit, heads, tokens)
    flows = [[send(first, to_right), None], [None, send(second, to_left)]]
    held, first = lax.optimization_barrier(([tuple(blocks[k]) for k in order], first))
    whole = assemble(held)
    sib_whole = send(whole, to_core)
    for k in range(far - 1, 0, -1):
        rows_at = [tokens * order.index(k), tokens * order.index(-k)]
        for i in (0, 1):
            sums = ring_sums(term[i], rows_at, flows[i])
            flows[i] = [send(sums[0], to_right), send(sums[1], to_left)]

    sib_dlogit = send(dlogit[ids:], to_core)
    grad_head = lax.dot_general(
        jnp.concatenate([dlogit[:ids], sib_dlogit], axis=1),
        jnp.concatenate([whole, sib_whole]),
        (((1,), (0,)), ((), ())),
        preferred_element_type=F32,
    ).astype(BF16)
    term, grad_head = lax.optimization_barrier((tuple(term), grad_head))
    grad_hidden = jnp.concatenate(
        [
            (t[:tokens] + f[0].astype(F32) + f[1].astype(F32)).astype(BF16)
            for t, f in zip(term, flows)
        ],
        axis=1,
    )
    return loss, grad_hidden, grad_head


def solution(mesh):
    devices = mesh.shape["pipe"]

    def per_device(*args):
        return program(devices, *args)

    placed = (
        P(("groups", "pipe"), None),
        P(("groups", "pipe"), None),
        P("groups", "pipe"),
        P("groups"),
        P("groups"),
    )
    return jax.shard_map(
        per_device,
        mesh=mesh,
        in_specs=placed,
        out_specs=(P(("groups", "pipe")), P(("groups", "pipe"), None), P(("groups", "pipe"), None)),
        check_vma=False,
    )
```

```python
import jax
import jax.numpy as jnp
from jax import lax
from jax.experimental import pallas as pl
from jax.experimental.pallas import tpu as pltpu
from jax.sharding import PartitionSpec as P

F32 = jnp.float32
BF16 = jnp.bfloat16


def chip_ring(chips):
    return list(range(0, chips, 2)) + list(reversed(range(1, chips, 2)))


def shift_pairs(ring, by):
    n = len(ring)
    return [(2 * ring[i] + c, 2 * ring[(i + by) % n] + c) for i in range(n) for c in (0, 1)]


def in_vmem(count):
    return [pl.BlockSpec(memory_space=pltpu.VMEM)] * count


def cost(flops, bytes_accessed, transcendentals):
    return pl.CostEstimate(
        flops=10 * flops, bytes_accessed=1 * bytes_accessed, transcendentals=transcendentals
    )


def kernel_params():
    return pltpu.CompilerParams(vmem_limit_bytes=12 * 2**20)


def stack_heads(own, sib):
    ids, width = own.shape

    def body(own_ref, sib_ref, out_ref, sem):
        copies = [
            pltpu.make_async_copy(own_ref, out_ref.at[0:ids], sem.at[0]),
            pltpu.make_async_copy(sib_ref, out_ref.at[ids : 2 * ids], sem.at[1]),
        ]
        for c in copies:
            c.start()
        for c in copies:
            c.wait()

    return pl.pallas_call(
        body,
        out_shape=pltpu.VMEM((2 * ids, width), own.dtype),
        in_specs=[pl.BlockSpec(memory_space=pl.ANY)] * 2,
        out_specs=in_vmem(1)[0],
        scratch_shapes=[pltpu.SemaphoreType.DMA((2,))],
        compiler_params=kernel_params(),
        cost_estimate=cost(
            flops=0, bytes_accessed=8 * ids * width, transcendentals=0
        ),
        name="stack_heads",
    )(own, sib)


def tile_of(width, most):
    tile = 128
    while tile * 2 <= most and width % (tile * 2) == 0:
        tile *= 2
    for factor in (3, 9):
        if tile * factor <= most and width % (tile * factor) == 0:
            return tile * factor
    return tile


def rows_of(group, start, size):
    parts = []
    for pieces in group:
        piece, at = pieces[0], start
        if start >= piece.shape[1]:
            piece, at = pieces[1], start - piece.shape[1]
        parts.append(piece[:, at : at + size])
    if len(parts) == 1:
        return parts[0]
    return jnp.concatenate([p.astype(F32) for p in parts]).astype(parts[0].dtype)


def whole_rows(group):
    return jnp.concatenate([jnp.concatenate(pieces, axis=1) for pieces in group])


def regroup(group, refs):
    refs = iter(refs)
    return [[next(refs) for _ in pieces] for pieces in group]


def logits(group, heads):
    tokens = group[0][0].shape[0]
    ids, width = heads.shape
    rows = tokens * len(group)
    if tokens % 8:
        return 3.0 * lax.dot_general(
            heads, whole_rows(group), (((1,), (1,)), ((), ())), preferred_element_type=F32
        )
    tile = tile_of(width // 2, 2304)
    flat = [x for pieces in group for x in pieces]

    def body(*refs):
        heads_ref, out_ref = refs[-2:]
        blocks = regroup(group, refs)
        acc = jnp.zeros((ids, rows), F32)
        for j in range(width // tile):
            x = rows_of(blocks, j * tile, tile)
            w = heads_ref[:, j * tile : (j + 1) * tile]
            acc += lax.dot_general(w, x, (((1,), (1,)), ((), ())), preferred_element_type=F32)
        out_ref[...] = 3.0 * acc

    return pl.pallas_call(
        body,
        out_shape=jax.ShapeDtypeStruct((ids, rows), F32),
        in_specs=in_vmem(len(flat) + 1),
        out_specs=in_vmem(1)[0],
        compiler_params=kernel_params(),
        cost_estimate=cost(
            flops=2 * ids * max(rows, 256) * width,
            bytes_accessed=2 * ids * width,
            transcendentals=0,
        ),
        name="logits",
    )(*flat, heads)


def assemble(group):
    tokens, dtype = group[0][0].shape[0], group[0][0].dtype
    rows = tokens * len(group)
    width = sum(x.shape[1] for x in group[0])
    if tokens % 8:
        return whole_rows(group)
    flat = [x for pieces in group for x in pieces]

    def body(*refs):
        out_ref = refs[-1]
        blocks = regroup(group, refs)
        for start in (0, width // 2):
            for i in range(0, len(blocks), 2):
                two = blocks[i : i + 2]
                out_ref[
                    tokens * i : tokens * (i + len(two)), start : start + width // 2
                ] = rows_of(two, start, width // 2)

    return pl.pallas_call(
        body,
        out_shape=pltpu.VMEM((rows, width), dtype),
        in_specs=in_vmem(len(flat)),
        out_specs=in_vmem(1)[0],
        compiler_params=kernel_params(),
        cost_estimate=cost(
            flops=0, bytes_accessed=4 * rows * width, transcendentals=0
        ),
        name="assemble",
    )(*flat)


def gradient_terms(dlogit, heads, late):
    ids, rows = dlogit.shape
    half = heads.shape[1] // 2
    early = rows - late
    if late % 8:
        term = lax.dot_general(dlogit, heads, (((0,), (0,)), ((), ())), preferred_element_type=F32)
        halves = term[:, :half], term[:, half:]
        return [h[:early] for h in halves] + [h[early:].astype(BF16) for h in halves]
    tile = tile_of(half, 1024)
    steps = half // tile

    def body(d_ref, heads_ref, *refs):
        d = d_ref[...].T
        for j in range(2 * steps):
            w = heads_ref[:, j * tile : (j + 1) * tile]
            term = jnp.dot(d, w, preferred_element_type=F32)
            cols = slice(j % steps * tile, (j % steps + 1) * tile)
            refs[j // steps][:, cols] = term[:early]
            refs[2 + j // steps][:, cols] = term[early:].astype(BF16)

    return pl.pallas_call(
        body,
        out_shape=[pltpu.VMEM((early, half), F32)] * 2 + [pltpu.VMEM((late, half), BF16)] * 2,
        in_specs=in_vmem(2),
        out_specs=in_vmem(4),
        compiler_params=kernel_params(),
        cost_estimate=cost(
            flops=2 * ids * 256 * 2 * half, bytes_accessed=4 * ids * half, transcendentals=0
        ),
        name="gradient_terms",
    )(dlogit, heads)


def ring_sums(term, rows, flows):
    half = term.shape[1]
    given = [f for f in flows if f is not None]
    tokens = given[0].shape[0]

    def total(own, flow):
        return (own if flow is None else own + flow.astype(F32)).astype(BF16)

    if tokens % 8:
        return [total(term[r : r + tokens], f) for r, f in zip(rows, flows)]

    def body(term_ref, *refs):
        came = iter(refs[: len(given)])
        for i in (0, 1):
            flow = None if flows[i] is None else next(came)[...]
            refs[len(given) + i][...] = total(term_ref[rows[i] : rows[i] + tokens, :], flow)

    return pl.pallas_call(
        body,
        out_shape=[jax.ShapeDtypeStruct((tokens, half), BF16)] * 2,
        in_specs=in_vmem(1 + len(given)),
        out_specs=in_vmem(2),
        compiler_params=kernel_params(),
        cost_estimate=cost(
            flops=2 * tokens * half, bytes_accessed=4 * tokens * half, transcendentals=0
        ),
        name="ring_sums",
    )(term, *given)


def local_stats(student, teach, onehot):
    sm = jnp.max(student, axis=0)
    tm = jnp.max(teach, axis=0)
    sexp = jnp.exp(student - sm)
    texp = jnp.exp(teach - tm)
    return jnp.stack(
        [
            sm,
            tm,
            jnp.sum(sexp, axis=0),
            jnp.sum(texp, axis=0),
            jnp.sum(texp * (teach - student), axis=0),
            jnp.sum(onehot * student, axis=0),
        ]
    )


def merge(every):
    sm = jnp.max(every[:, 0], axis=0)
    tm = jnp.max(every[:, 1], axis=0)
    s = jnp.exp(every[:, 0] - sm)
    t = jnp.exp(every[:, 1] - tm)
    return (
        sm,
        tm,
        jnp.sum(every[:, 2] * s, axis=0),
        jnp.sum(every[:, 3] * t, axis=0),
        jnp.sum(every[:, 4] * t, axis=0),
        jnp.sum(every[:, 5], axis=0),
    )


def from_every_chip(x, ring):
    n = len(ring)
    known = x[None]
    reach = 0
    while known.shape[0] < n:
        width = 2 * reach + 1
        missing = n - width
        right = min(width, (missing + 1) // 2)
        left = min(width, missing - right)
        ahead = lax.ppermute(known[:right], "pipe", shift_pairs(ring, -width))
        parts = [known, ahead]
        if left:
            parts.insert(0, lax.ppermute(known[width - left :], "pipe", shift_pairs(ring, width)))
        known = jnp.concatenate(parts)
        reach = 3 * reach + 1
    return known


def program(devices, hidden, head_rows, teacher, targets, token_weight):
    chips = devices // 2
    ring = chip_ring(chips)
    far = chips // 2
    tokens, width = hidden.shape
    half = width // 2
    ids = head_rows.shape[0]

    me = lax.axis_index("pipe")
    core = me % 2
    chip = me // 2
    place = jnp.where(chip % 2 == 0, chip // 2, chips - 1 - chip // 2)
    to_core = [(i, i ^ 1) for i in range(devices)]
    to_right, to_left = shift_pairs(ring, 1), shift_pairs(ring, -1)

    def send(x, perm):
        return lax.ppermute(x, "pipe", perm)

    sib_head = send(head_rows, to_core)
    heads = stack_heads(head_rows, sib_head)

    blocks = {0: hidden}
    for k in range(1, far):
        behind, ahead = blocks[1 - k], blocks[k - 1]
        if k == far - 1:
            behind, ahead, heads = lax.optimization_barrier((behind, ahead, heads))
        blocks[-k] = send(behind, to_right)
        blocks[k] = send(ahead, to_left)
    order = list(range(0, far)) + list(range(1 - far, 0)) + [far]
    order = [0] + [s * k for k in range(1, far) for s in (1, -1)] + [far]
    near = [k for k in order if abs(k) < far - 1]
    early = logits([[blocks[k]] for k in near], heads)
    rest = [k for k in order if k not in near and k != far]
    edge_left, edge_right, early = lax.optimization_barrier((blocks[1 - far], blocks[far - 1], early))
    last = (send(edge_left[:, :half], to_right), send(edge_right[:, half:], to_left))
    blocks = {k: [x] for k, x in blocks.items()}
    blocks[far] = last
    parts = [early, logits([blocks[k] for k in rest], heads), logits([blocks[far]], heads)]
    rows = len(order) * tokens

    steps = jnp.array(order, jnp.int32)
    at = (place + steps) % chips
    row_chip = jnp.where(at < chips // 2, 2 * at, 2 * (chips - 1 - at) + 1)
    inner = jnp.arange(tokens, dtype=jnp.int32)[None, :]
    row_token = (((2 * row_chip + core) * tokens)[:, None] + inner).reshape(rows)
    row_slot = ((row_chip * tokens)[:, None] + inner).reshape(rows)
    select = row_token[:, None] == jnp.arange(devices * tokens, dtype=jnp.int32)[None, :]
    slots = (row_slot[:, None] == jnp.arange(rows, dtype=jnp.int32)[None, :]).astype(F32)

    def pick(x):
        return jnp.sum(jnp.where(select, x[None, :], 0), axis=1, dtype=x.dtype)

    both_teacher = jnp.concatenate([teacher, send(teacher, to_core)], axis=1)
    teach = lax.dot_general(
        both_teacher, select.astype(BF16), (((0,), (1,)), ((), ())), preferred_element_type=F32
    )
    target = pick(targets)
    weight = pick(token_weight)
    lanes = jnp.arange(ids, dtype=jnp.int32)
    columns = jnp.concatenate([me * ids + lanes, (me ^ 1) * ids + lanes])
    onehot = (columns[:, None] == target[None, :]).astype(F32)

    student = jnp.concatenate(parts, axis=1)
    exact = lax.Precision.HIGHEST
    stats = jnp.dot(local_stats(student, teach, onehot), slots, precision=exact)
    merged = jnp.stack(merge(from_every_chip(stats, ring)))
    smax, tmax, szero, tzero, cross, picked = lax.dot_general(
        merged, slots, (((1,), (1,)), ((), ())), precision=exact
    )
    loss_rows = cross / tzero - (tmax + jnp.log(tzero)) + 2.0 * (smax + jnp.log(szero)) - picked
    loss = loss_rows[:tokens]

    sexp = jnp.exp(student - smax)
    texp = jnp.exp(teach - tmax)
    dlogit = (3.0 * weight * (2.0 * sexp / szero - texp / tzero - onehot)).astype(BF16)

    *term, first, second = gradient_terms(dlogit, heads, tokens)
    flows = [[send(first, to_right), None], [None, send(second, to_left)]]
    held, first = lax.optimization_barrier(([tuple(blocks[k]) for k in order], first))
    whole = assemble(held)
    sib_whole = send(whole, to_core)
    for k in range(far - 1, 0, -1):
        rows_at = [tokens * order.index(k), tokens * order.index(-k)]
        for i in (0, 1):
            sums = ring_sums(term[i], rows_at, flows[i])
            flows[i] = [send(sums[0], to_right), send(sums[1], to_left)]

    sib_dlogit = send(dlogit[ids:], to_core)
    grad_head = lax.dot_general(
        jnp.concatenate([dlogit[:ids], sib_dlogit], axis=1),
        jnp.concatenate([whole, sib_whole]),
        (((1,), (0,)), ((), ())),
        preferred_element_type=F32,
    ).astype(BF16)
    term, grad_head = lax.optimization_barrier((tuple(term), grad_head))
    grad_hidden = jnp.concatenate(
        [
            (t[:tokens] + f[0].astype(F32) + f[1].astype(F32)).astype(BF16)
            for t, f in zip(term, flows)
        ],
        axis=1,
    )
    return loss, grad_hidden, grad_head


def solution(mesh):
    devices = mesh.shape["pipe"]

    def per_device(*args):
        return program(devices, *args)

    placed = (
        P(("groups", "pipe"), None),
        P(("groups", "pipe"), None),
        P("groups", "pipe"),
        P("groups"),
        P("groups"),
    )
    return jax.shard_map(
        per_device,
        mesh=mesh,
        in_specs=placed,
        out_specs=(P(("groups", "pipe")), P(("groups", "pipe"), None), P(("groups", "pipe"), None)),
        check_vma=False,
    )
```

```python
import jax
import jax.numpy as jnp
from jax import lax
from jax.experimental import pallas as pl
from jax.experimental.pallas import tpu as pltpu
from jax.sharding import PartitionSpec as P

F32 = jnp.float32
BF16 = jnp.bfloat16


def chip_ring(chips):
    return list(range(0, chips, 2)) + list(reversed(range(1, chips, 2)))


def shift_pairs(ring, by):
    n = len(ring)
    return [(2 * ring[i] + c, 2 * ring[(i + by) % n] + c) for i in range(n) for c in (0, 1)]


def in_vmem(count):
    return [pl.BlockSpec(memory_space=pltpu.VMEM)] * count


def cost(flops, bytes_accessed, transcendentals):
    return pl.CostEstimate(
        flops=10 * flops, bytes_accessed=1 * bytes_accessed, transcendentals=transcendentals
    )


def kernel_params():
    return pltpu.CompilerParams(vmem_limit_bytes=12 * 2**20)


def stack_heads(own, sib):
    ids, width = own.shape

    def body(own_ref, sib_ref, out_ref, sem):
        copies = [
            pltpu.make_async_copy(own_ref, out_ref.at[0:ids], sem.at[0]),
            pltpu.make_async_copy(sib_ref, out_ref.at[ids : 2 * ids], sem.at[1]),
        ]
        for c in copies:
            c.start()
        for c in copies:
            c.wait()

    return pl.pallas_call(
        body,
        out_shape=pltpu.VMEM((2 * ids, width), own.dtype),
        in_specs=[pl.BlockSpec(memory_space=pl.ANY)] * 2,
        out_specs=in_vmem(1)[0],
        scratch_shapes=[pltpu.SemaphoreType.DMA((2,))],
        compiler_params=kernel_params(),
        cost_estimate=cost(
            flops=0, bytes_accessed=8 * ids * width, transcendentals=0
        ),
        name="stack_heads",
    )(own, sib)


def tile_of(width, most):
    tile = 128
    while tile * 2 <= most and width % (tile * 2) == 0:
        tile *= 2
    for factor in (3, 9):
        if tile * factor <= most and width % (tile * factor) == 0:
            return tile * factor
    return tile


def rows_of(group, start, size):
    parts = []
    for pieces in group:
        piece, at = pieces[0], start
        if start >= piece.shape[1]:
            piece, at = pieces[1], start - piece.shape[1]
        parts.append(piece[:, at : at + size])
    if len(parts) == 1:
        return parts[0]
    return jnp.concatenate([p.astype(F32) for p in parts]).astype(parts[0].dtype)


def whole_rows(group):
    return jnp.concatenate([jnp.concatenate(pieces, axis=1) for pieces in group])


def regroup(group, refs):
    refs = iter(refs)
    return [[next(refs) for _ in pieces] for pieces in group]


def logits(group, heads):
    tokens = group[0][0].shape[0]
    ids, width = heads.shape
    rows = tokens * len(group)
    if tokens % 8:
        return 3.0 * lax.dot_general(
            heads, whole_rows(group), (((1,), (1,)), ((), ())), preferred_element_type=F32
        )
    tile = tile_of(width // 2, 2304)
    flat = [x for pieces in group for x in pieces]

    def body(*refs):
        heads_ref, out_ref = refs[-2:]
        blocks = regroup(group, refs)
        acc = jnp.zeros((ids, rows), F32)
        for j in range(width // tile):
            x = rows_of(blocks, j * tile, tile)
            w = heads_ref[:, j * tile : (j + 1) * tile]
            acc += lax.dot_general(w, x, (((1,), (1,)), ((), ())), preferred_element_type=F32)
        out_ref[...] = 3.0 * acc

    return pl.pallas_call(
        body,
        out_shape=jax.ShapeDtypeStruct((ids, rows), F32),
        in_specs=in_vmem(len(flat) + 1),
        out_specs=in_vmem(1)[0],
        compiler_params=kernel_params(),
        cost_estimate=cost(
            flops=2 * ids * max(rows, 256) * width,
            bytes_accessed=2 * ids * width,
            transcendentals=0,
        ),
        name="logits",
    )(*flat, heads)


def assemble(group):
    tokens, dtype = group[0][0].shape[0], group[0][0].dtype
    rows = tokens * len(group)
    width = sum(x.shape[1] for x in group[0])
    if tokens % 8:
        return whole_rows(group)
    flat = [x for pieces in group for x in pieces]

    def body(*refs):
        out_ref = refs[-1]
        blocks = regroup(group, refs)
        for start in (0, width // 2):
            for i in range(0, len(blocks), 2):
                two = blocks[i : i + 2]
                out_ref[
                    tokens * i : tokens * (i + len(two)), start : start + width // 2
                ] = rows_of(two, start, width // 2)

    return pl.pallas_call(
        body,
        out_shape=pltpu.VMEM((rows, width), dtype),
        in_specs=in_vmem(len(flat)),
        out_specs=in_vmem(1)[0],
        compiler_params=kernel_params(),
        cost_estimate=cost(
            flops=0, bytes_accessed=4 * rows * width, transcendentals=0
        ),
        name="assemble",
    )(*flat)


def gradient_terms(dlogit, heads, late):
    ids, rows = dlogit.shape
    half = heads.shape[1] // 2
    early = rows - late
    if late % 8:
        term = lax.dot_general(dlogit, heads, (((0,), (0,)), ((), ())), preferred_element_type=F32)
        halves = term[:, :half], term[:, half:]
        return [h[:early] for h in halves] + [h[early:].astype(BF16) for h in halves]
    tile = tile_of(half, 1024)
    steps = half // tile

    def body(d_ref, heads_ref, *refs):
        d = d_ref[...].T
        for j in range(2 * steps):
            w = heads_ref[:, j * tile : (j + 1) * tile]
            term = jnp.dot(d, w, preferred_element_type=F32)
            cols = slice(j % steps * tile, (j % steps + 1) * tile)
            refs[j // steps][:, cols] = term[:early]
            refs[2 + j // steps][:, cols] = term[early:].astype(BF16)

    return pl.pallas_call(
        body,
        out_shape=[pltpu.VMEM((early, half), F32)] * 2 + [pltpu.VMEM((late, half), BF16)] * 2,
        in_specs=in_vmem(2),
        out_specs=in_vmem(4),
        compiler_params=kernel_params(),
        cost_estimate=cost(
            flops=2 * ids * 256 * 2 * half, bytes_accessed=4 * ids * half, transcendentals=0
        ),
        name="gradient_terms",
    )(dlogit, heads)


def ring_sums(term, rows, flows):
    half = term.shape[1]
    given = [f for f in flows if f is not None]
    tokens = given[0].shape[0]

    def total(own, flow):
        return (own if flow is None else own + flow.astype(F32)).astype(BF16)

    if tokens % 8:
        return [total(term[r : r + tokens], f) for r, f in zip(rows, flows)]

    def body(term_ref, *refs):
        came = iter(refs[: len(given)])
        for i in (0, 1):
            flow = None if flows[i] is None else next(came)[...]
            refs[len(given) + i][...] = total(term_ref[rows[i] : rows[i] + tokens, :], flow)

    return pl.pallas_call(
        body,
        out_shape=[jax.ShapeDtypeStruct((tokens, half), BF16)] * 2,
        in_specs=in_vmem(1 + len(given)),
        out_specs=in_vmem(2),
        compiler_params=kernel_params(),
        cost_estimate=cost(
            flops=2 * tokens * half, bytes_accessed=4 * tokens * half, transcendentals=0
        ),
        name="ring_sums",
    )(term, *given)


def local_stats(student, teach, onehot):
    sm = jnp.max(student, axis=0)
    tm = jnp.max(teach, axis=0)
    sexp = jnp.exp(student - sm)
    texp = jnp.exp(teach - tm)
    return jnp.stack(
        [
            sm,
            tm,
            jnp.sum(sexp, axis=0),
            jnp.sum(texp, axis=0),
            jnp.sum(texp * (teach - student), axis=0),
            jnp.sum(onehot * student, axis=0),
        ]
    )


def merge(every):
    sm = jnp.max(every[:, 0], axis=0)
    tm = jnp.max(every[:, 1], axis=0)
    s = jnp.exp(every[:, 0] - sm)
    t = jnp.exp(every[:, 1] - tm)
    return (
        sm,
        tm,
        jnp.sum(every[:, 2] * s, axis=0),
        jnp.sum(every[:, 3] * t, axis=0),
        jnp.sum(every[:, 4] * t, axis=0),
        jnp.sum(every[:, 5], axis=0),
    )


def from_every_chip(x, ring):
    n = len(ring)
    known = x[None]
    reach = 0
    while known.shape[0] < n:
        width = 2 * reach + 1
        missing = n - width
        right = min(width, (missing + 1) // 2)
        left = min(width, missing - right)
        ahead = lax.ppermute(known[:right], "pipe", shift_pairs(ring, -width))
        parts = [known, ahead]
        if left:
            parts.insert(0, lax.ppermute(known[width - left :], "pipe", shift_pairs(ring, width)))
        known = jnp.concatenate(parts)
        reach = 3 * reach + 1
    return known


def program(devices, hidden, head_rows, teacher, targets, token_weight):
    chips = devices // 2
    ring = chip_ring(chips)
    far = chips // 2
    tokens, width = hidden.shape
    half = width // 2
    ids = head_rows.shape[0]

    me = lax.axis_index("pipe")
    core = me % 2
    chip = me // 2
    place = jnp.where(chip % 2 == 0, chip // 2, chips - 1 - chip // 2)
    to_core = [(i, i ^ 1) for i in range(devices)]
    to_right, to_left = shift_pairs(ring, 1), shift_pairs(ring, -1)

    def send(x, perm):
        return lax.ppermute(x, "pipe", perm)

    sib_head = send(head_rows, to_core)
    heads = stack_heads(head_rows, sib_head)

    blocks = {0: hidden}
    for k in range(1, far):
        behind, ahead = blocks[1 - k], blocks[k - 1]
        if k == far - 1:
            behind, ahead, heads = lax.optimization_barrier((behind, ahead, heads))
        blocks[-k] = send(behind, to_right)
        blocks[k] = send(ahead, to_left)
    order = list(range(0, far)) + list(range(1 - far, 0)) + [far]
    order = [0] + [s * k for k in range(1, far) for s in (1, -1)] + [far]
    near = [k for k in order if abs(k) < far - 1]
    early = logits([[blocks[k]] for k in near], heads)
    rest = [k for k in order if k not in near and k != far]
    edge_left, early = lax.optimization_barrier((blocks[1 - far], early))
    edge_right = blocks[far - 1]
    last = (send(edge_left[:, :half], to_right), send(edge_right[:, half:], to_left))
    blocks = {k: [x] for k, x in blocks.items()}
    blocks[far] = last
    parts = [early, logits([blocks[k] for k in rest], heads), logits([blocks[far]], heads)]
    rows = len(order) * tokens

    steps = jnp.array(order, jnp.int32)
    at = (place + steps) % chips
    row_chip = jnp.where(at < chips // 2, 2 * at, 2 * (chips - 1 - at) + 1)
    inner = jnp.arange(tokens, dtype=jnp.int32)[None, :]
    row_token = (((2 * row_chip + core) * tokens)[:, None] + inner).reshape(rows)
    row_slot = ((row_chip * tokens)[:, None] + inner).reshape(rows)
    select = row_token[:, None] == jnp.arange(devices * tokens, dtype=jnp.int32)[None, :]
    slots = (row_slot[:, None] == jnp.arange(rows, dtype=jnp.int32)[None, :]).astype(F32)

    def pick(x):
        return jnp.sum(jnp.where(select, x[None, :], 0), axis=1, dtype=x.dtype)

    both_teacher = jnp.concatenate([teacher, send(teacher, to_core)], axis=1)
    teach = lax.dot_general(
        both_teacher, select.astype(BF16), (((0,), (1,)), ((), ())), preferred_element_type=F32
    )
    target = pick(targets)
    weight = pick(token_weight)
    lanes = jnp.arange(ids, dtype=jnp.int32)
    columns = jnp.concatenate([me * ids + lanes, (me ^ 1) * ids + lanes])
    onehot = (columns[:, None] == target[None, :]).astype(F32)

    student = jnp.concatenate(parts, axis=1)
    exact = lax.Precision.HIGHEST
    stats = jnp.dot(local_stats(student, teach, onehot), slots, precision=exact)
    merged = jnp.stack(merge(from_every_chip(stats, ring)))
    smax, tmax, szero, tzero, cross, picked = lax.dot_general(
        merged, slots, (((1,), (1,)), ((), ())), precision=exact
    )
    loss_rows = cross / tzero - (tmax + jnp.log(tzero)) + 2.0 * (smax + jnp.log(szero)) - picked
    loss = loss_rows[:tokens]

    sexp = jnp.exp(student - smax)
    texp = jnp.exp(teach - tmax)
    dlogit = (3.0 * weight * (2.0 * sexp / szero - texp / tzero - onehot)).astype(BF16)

    *term, first, second = gradient_terms(dlogit, heads, tokens)
    flows = [[send(first, to_right), None], [None, send(second, to_left)]]
    held, first = lax.optimization_barrier(([tuple(blocks[k]) for k in order], first))
    whole = assemble(held)
    sib_whole = send(whole, to_core)
    for k in range(far - 1, 0, -1):
        rows_at = [tokens * order.index(k), tokens * order.index(-k)]
        for i in (0, 1):
            sums = ring_sums(term[i], rows_at, flows[i])
            flows[i] = [send(sums[0], to_right), send(sums[1], to_left)]

    sib_dlogit = send(dlogit[ids:], to_core)
    grad_head = lax.dot_general(
        jnp.concatenate([dlogit[:ids], sib_dlogit], axis=1),
        jnp.concatenate([whole, sib_whole]),
        (((1,), (0,)), ((), ())),
        preferred_element_type=F32,
    ).astype(BF16)
    term, grad_head = lax.optimization_barrier((tuple(term), grad_head))
    grad_hidden = jnp.concatenate(
        [
            (t[:tokens] + f[0].astype(F32) + f[1].astype(F32)).astype(BF16)
            for t, f in zip(term, flows)
        ],
        axis=1,
    )
    return loss, grad_hidden, grad_head


def solution(mesh):
    devices = mesh.shape["pipe"]

    def per_device(*args):
        return program(devices, *args)

    placed = (
        P(("groups", "pipe"), None),
        P(("groups", "pipe"), None),
        P("groups", "pipe"),
        P("groups"),
        P("groups"),
    )
    return jax.shard_map(
        per_device,
        mesh=mesh,
        in_specs=placed,
        out_specs=(P(("groups", "pipe")), P(("groups", "pipe"), None), P(("groups", "pipe"), None)),
        check_vma=False,
    )
```

```python
import jax
import jax.numpy as jnp
from jax import lax
from jax.experimental import pallas as pl
from jax.experimental.pallas import tpu as pltpu
from jax.sharding import PartitionSpec as P

F32 = jnp.float32
BF16 = jnp.bfloat16


def chip_ring(chips):
    return list(range(0, chips, 2)) + list(reversed(range(1, chips, 2)))


def shift_pairs(ring, by):
    n = len(ring)
    return [(2 * ring[i] + c, 2 * ring[(i + by) % n] + c) for i in range(n) for c in (0, 1)]


def in_vmem(count):
    return [pl.BlockSpec(memory_space=pltpu.VMEM)] * count


def cost(flops, bytes_accessed, transcendentals):
    return pl.CostEstimate(
        flops=10 * flops, bytes_accessed=1 * bytes_accessed, transcendentals=transcendentals
    )


def kernel_params():
    return pltpu.CompilerParams(vmem_limit_bytes=12 * 2**20)


def stack_heads(own, sib):
    ids, width = own.shape

    def body(own_ref, sib_ref, out_ref, sem):
        copies = [
            pltpu.make_async_copy(own_ref, out_ref.at[0:ids], sem.at[0]),
            pltpu.make_async_copy(sib_ref, out_ref.at[ids : 2 * ids], sem.at[1]),
        ]
        for c in copies:
            c.start()
        for c in copies:
            c.wait()

    return pl.pallas_call(
        body,
        out_shape=pltpu.VMEM((2 * ids, width), own.dtype),
        in_specs=[pl.BlockSpec(memory_space=pl.ANY)] * 2,
        out_specs=in_vmem(1)[0],
        scratch_shapes=[pltpu.SemaphoreType.DMA((2,))],
        compiler_params=kernel_params(),
        cost_estimate=cost(
            flops=0, bytes_accessed=8 * ids * width, transcendentals=0
        ),
        name="stack_heads",
    )(own, sib)


def tile_of(width, most):
    tile = 128
    while tile * 2 <= most and width % (tile * 2) == 0:
        tile *= 2
    for factor in (3, 9):
        if tile * factor <= most and width % (tile * factor) == 0:
            return tile * factor
    return tile


def rows_of(group, start, size):
    parts = []
    for pieces in group:
        piece, at = pieces[0], start
        if start >= piece.shape[1]:
            piece, at = pieces[1], start - piece.shape[1]
        parts.append(piece[:, at : at + size])
    if len(parts) == 1:
        return parts[0]
    return jnp.concatenate([p.astype(F32) for p in parts]).astype(parts[0].dtype)


def whole_rows(group):
    return jnp.concatenate([jnp.concatenate(pieces, axis=1) for pieces in group])


def regroup(group, refs):
    refs = iter(refs)
    return [[next(refs) for _ in pieces] for pieces in group]


def logits(group, heads):
    tokens = group[0][0].shape[0]
    ids, width = heads.shape
    rows = tokens * len(group)
    if tokens % 8:
        return 3.0 * lax.dot_general(
            heads, whole_rows(group), (((1,), (1,)), ((), ())), preferred_element_type=F32
        )
    tile = tile_of(width // 2, 2304)
    flat = [x for pieces in group for x in pieces]

    def body(*refs):
        heads_ref, out_ref = refs[-2:]
        blocks = regroup(group, refs)
        acc = jnp.zeros((ids, rows), F32)
        for j in range(width // tile):
            x = rows_of(blocks, j * tile, tile)
            w = heads_ref[:, j * tile : (j + 1) * tile]
            acc += lax.dot_general(w, x, (((1,), (1,)), ((), ())), preferred_element_type=F32)
        out_ref[...] = 3.0 * acc

    return pl.pallas_call(
        body,
        out_shape=jax.ShapeDtypeStruct((ids, rows), F32),
        in_specs=in_vmem(len(flat) + 1),
        out_specs=in_vmem(1)[0],
        compiler_params=kernel_params(),
        cost_estimate=cost(
            flops=2 * ids * max(rows, 256) * width,
            bytes_accessed=2 * ids * width,
            transcendentals=0,
        ),
        name="logits",
    )(*flat, heads)


def assemble(group):
    tokens, dtype = group[0][0].shape[0], group[0][0].dtype
    rows = tokens * len(group)
    width = sum(x.shape[1] for x in group[0])
    if tokens % 8:
        return whole_rows(group)
    flat = [x for pieces in group for x in pieces]

    def body(*refs):
        out_ref = refs[-1]
        blocks = regroup(group, refs)
        for start in (0, width // 2):
            for i in range(0, len(blocks), 2):
                two = blocks[i : i + 2]
                out_ref[
                    tokens * i : tokens * (i + len(two)), start : start + width // 2
                ] = rows_of(two, start, width // 2)

    return pl.pallas_call(
        body,
        out_shape=pltpu.VMEM((rows, width), dtype),
        in_specs=in_vmem(len(flat)),
        out_specs=in_vmem(1)[0],
        compiler_params=kernel_params(),
        cost_estimate=cost(
            flops=0, bytes_accessed=4 * rows * width, transcendentals=0
        ),
        name="assemble",
    )(*flat)


def gradient_terms(dlogit, heads, late):
    ids, rows = dlogit.shape
    half = heads.shape[1] // 2
    early = rows - late
    if late % 8:
        term = lax.dot_general(dlogit, heads, (((0,), (0,)), ((), ())), preferred_element_type=F32)
        halves = term[:, :half], term[:, half:]
        return [h[:early] for h in halves] + [h[early:].astype(BF16) for h in halves]
    tile = tile_of(half, 1024)
    steps = half // tile

    def body(d_ref, heads_ref, *refs):
        d = d_ref[...].T
        for j in range(2 * steps):
            w = heads_ref[:, j * tile : (j + 1) * tile]
            term = jnp.dot(d, w, preferred_element_type=F32)
            cols = slice(j % steps * tile, (j % steps + 1) * tile)
            refs[j // steps][:, cols] = term[:early]
            refs[2 + j // steps][:, cols] = term[early:].astype(BF16)

    return pl.pallas_call(
        body,
        out_shape=[pltpu.VMEM((early, half), F32)] * 2 + [pltpu.VMEM((late, half), BF16)] * 2,
        in_specs=in_vmem(2),
        out_specs=in_vmem(4),
        compiler_params=kernel_params(),
        cost_estimate=cost(
            flops=2 * ids * 256 * 2 * half, bytes_accessed=4 * ids * half, transcendentals=0
        ),
        name="gradient_terms",
    )(dlogit, heads)


def ring_sums(term, rows, flows):
    half = term.shape[1]
    given = [f for f in flows if f is not None]
    tokens = given[0].shape[0]

    def total(own, flow):
        return (own if flow is None else own + flow.astype(F32)).astype(BF16)

    if tokens % 8:
        return [total(term[r : r + tokens], f) for r, f in zip(rows, flows)]

    def body(term_ref, *refs):
        came = iter(refs[: len(given)])
        for i in (0, 1):
            flow = None if flows[i] is None else next(came)[...]
            refs[len(given) + i][...] = total(term_ref[rows[i] : rows[i] + tokens, :], flow)

    return pl.pallas_call(
        body,
        out_shape=[jax.ShapeDtypeStruct((tokens, half), BF16)] * 2,
        in_specs=in_vmem(1 + len(given)),
        out_specs=in_vmem(2),
        compiler_params=kernel_params(),
        cost_estimate=cost(
            flops=200 * tokens * half, bytes_accessed=4 * tokens * half, transcendentals=0
        ),
        name="ring_sums",
    )(term, *given)


def local_stats(student, teach, onehot):
    sm = jnp.max(student, axis=0)
    tm = jnp.max(teach, axis=0)
    sexp = jnp.exp(student - sm)
    texp = jnp.exp(teach - tm)
    return jnp.stack(
        [
            sm,
            tm,
            jnp.sum(sexp, axis=0),
            jnp.sum(texp, axis=0),
            jnp.sum(texp * (teach - student), axis=0),
            jnp.sum(onehot * student, axis=0),
        ]
    )


def merge(every):
    sm = jnp.max(every[:, 0], axis=0)
    tm = jnp.max(every[:, 1], axis=0)
    s = jnp.exp(every[:, 0] - sm)
    t = jnp.exp(every[:, 1] - tm)
    return (
        sm,
        tm,
        jnp.sum(every[:, 2] * s, axis=0),
        jnp.sum(every[:, 3] * t, axis=0),
        jnp.sum(every[:, 4] * t, axis=0),
        jnp.sum(every[:, 5], axis=0),
    )


def from_every_chip(x, ring):
    n = len(ring)
    known = x[None]
    reach = 0
    while known.shape[0] < n:
        width = 2 * reach + 1
        missing = n - width
        right = min(width, (missing + 1) // 2)
        left = min(width, missing - right)
        ahead = lax.ppermute(known[:right], "pipe", shift_pairs(ring, -width))
        parts = [known, ahead]
        if left:
            parts.insert(0, lax.ppermute(known[width - left :], "pipe", shift_pairs(ring, width)))
        known = jnp.concatenate(parts)
        reach = 3 * reach + 1
    return known


def program(devices, hidden, head_rows, teacher, targets, token_weight):
    chips = devices // 2
    ring = chip_ring(chips)
    far = chips // 2
    tokens, width = hidden.shape
    half = width // 2
    ids = head_rows.shape[0]

    me = lax.axis_index("pipe")
    core = me % 2
    chip = me // 2
    place = jnp.where(chip % 2 == 0, chip // 2, chips - 1 - chip // 2)
    to_core = [(i, i ^ 1) for i in range(devices)]
    to_right, to_left = shift_pairs(ring, 1), shift_pairs(ring, -1)

    def send(x, perm):
        return lax.ppermute(x, "pipe", perm)

    sib_head = send(head_rows, to_core)
    heads = stack_heads(head_rows, sib_head)

    blocks = {0: hidden}
    for k in range(1, far):
        behind, ahead = blocks[1 - k], blocks[k - 1]
        if k == far - 1:
            behind, ahead, heads = lax.optimization_barrier((behind, ahead, heads))
        blocks[-k] = send(behind, to_right)
        blocks[k] = send(ahead, to_left)
    order = list(range(0, far)) + list(range(1 - far, 0)) + [far]
    order = [0] + [s * k for k in range(1, far) for s in (1, -1)] + [far]
    near = [k for k in order if abs(k) < far - 1]
    early = logits([[blocks[k]] for k in near], heads)
    rest = [k for k in order if k not in near and k != far]
    edge_left, early = lax.optimization_barrier((blocks[1 - far], early))
    edge_right = blocks[far - 1]
    last = (send(edge_left[:, :half], to_right), send(edge_right[:, half:], to_left))
    blocks = {k: [x] for k, x in blocks.items()}
    blocks[far] = last
    parts = [early, logits([blocks[k] for k in rest], heads), logits([blocks[far]], heads)]
    rows = len(order) * tokens

    steps = jnp.array(order, jnp.int32)
    at = (place + steps) % chips
    row_chip = jnp.where(at < chips // 2, 2 * at, 2 * (chips - 1 - at) + 1)
    inner = jnp.arange(tokens, dtype=jnp.int32)[None, :]
    row_token = (((2 * row_chip + core) * tokens)[:, None] + inner).reshape(rows)
    row_slot = ((row_chip * tokens)[:, None] + inner).reshape(rows)
    select = row_token[:, None] == jnp.arange(devices * tokens, dtype=jnp.int32)[None, :]
    slots = (row_slot[:, None] == jnp.arange(rows, dtype=jnp.int32)[None, :]).astype(F32)

    def pick(x):
        return jnp.sum(jnp.where(select, x[None, :], 0), axis=1, dtype=x.dtype)

    both_teacher = jnp.concatenate([teacher, send(teacher, to_core)], axis=1)
    teach = lax.dot_general(
        both_teacher, select.astype(BF16), (((0,), (1,)), ((), ())), preferred_element_type=F32
    )
    target = pick(targets)
    weight = pick(token_weight)
    lanes = jnp.arange(ids, dtype=jnp.int32)
    columns = jnp.concatenate([me * ids + lanes, (me ^ 1) * ids + lanes])
    onehot = (columns[:, None] == target[None, :]).astype(F32)

    student = jnp.concatenate(parts, axis=1)
    exact = lax.Precision.HIGHEST
    stats = jnp.dot(local_stats(student, teach, onehot), slots, precision=exact)
    merged = jnp.stack(merge(from_every_chip(stats, ring)))
    smax, tmax, szero, tzero, cross, picked = lax.dot_general(
        merged, slots, (((1,), (1,)), ((), ())), precision=exact
    )
    loss_rows = cross / tzero - (tmax + jnp.log(tzero)) + 2.0 * (smax + jnp.log(szero)) - picked
    loss = loss_rows[:tokens]

    sexp = jnp.exp(student - smax)
    texp = jnp.exp(teach - tmax)
    dlogit = (3.0 * weight * (2.0 * sexp / szero - texp / tzero - onehot)).astype(BF16)

    *term, first, second = gradient_terms(dlogit, heads, tokens)
    flows = [[send(first, to_right), None], [None, send(second, to_left)]]
    held, first = lax.optimization_barrier(([tuple(blocks[k]) for k in order], first))
    whole = assemble(held)
    sib_whole = send(whole, to_core)
    for k in range(far - 1, 0, -1):
        rows_at = [tokens * order.index(k), tokens * order.index(-k)]
        for i in (0, 1):
            sums = ring_sums(term[i], rows_at, flows[i])
            flows[i] = [send(sums[0], to_right), send(sums[1], to_left)]

    sib_dlogit = send(dlogit[ids:], to_core)
    grad_head = lax.dot_general(
        jnp.concatenate([dlogit[:ids], sib_dlogit], axis=1),
        jnp.concatenate([whole, sib_whole]),
        (((1,), (0,)), ((), ())),
        preferred_element_type=F32,
    ).astype(BF16)
    term, grad_head = lax.optimization_barrier((tuple(term), grad_head))
    grad_hidden = jnp.concatenate(
        [
            (t[:tokens] + f[0].astype(F32) + f[1].astype(F32)).astype(BF16)
            for t, f in zip(term, flows)
        ],
        axis=1,
    )
    return loss, grad_hidden, grad_head


def solution(mesh):
    devices = mesh.shape["pipe"]

    def per_device(*args):
        return program(devices, *args)

    placed = (
        P(("groups", "pipe"), None),
        P(("groups", "pipe"), None),
        P("groups", "pipe"),
        P("groups"),
        P("groups"),
    )
    return jax.shard_map(
        per_device,
        mesh=mesh,
        in_specs=placed,
        out_specs=(P(("groups", "pipe")), P(("groups", "pipe"), None), P(("groups", "pipe"), None)),
        check_vma=False,
    )
```
